32 devices in a mesh: fold: 4 (over y, x), trow: 4 (over z), tcol: 2 (over core).
Axes of the slice: x: 2, y: 2, z: 4, core: 2. Of those that a mesh axis runs over, the one named last changes fastest.
Arguments:
- samples: bfloat16 [8, 2048, 256], P('fold', ('trow', 'tcol')), may hold values from -6 to 6
- targets: bfloat16 [8, 2048, 128], P('fold', ('trow', 'tcol')), may hold values from -6 to 6
- frequencies: bfloat16 [256, 4096], replicated, may hold values from -1.5 to 1.5
- phases: float32 [4096], replicated, may hold values from -3.140625 to 3.140625
- valid_rows: int32 [8], P('fold'), may hold values from 1024 to 2048
- ridge: float32 [8], P('fold'), may hold values from 0.1 to 1
- low_bound: float32 [8], P('fold'), may hold values from 0.05 to 0.4
- high_bound: float32 [8], P('fold'), may hold values from 9 to 12
Outputs:
- iterate: float32 [8, 4096, 128], P('fold', 'tcol')
- residual: float32 [8, 4096, 128], P('fold', 'tcol')
The draws below stay inside these ranges and needn't reach their ends.
Inputs may be any that keep to these rules, and one draw needn't show every extreme that they name: Rows of fold k at positions valid_rows[k] and beyond take no part in any fit.
All inputs are finite; a program needn't handle non-finite values.
Results may differ from the reference program's by a relative error of at most 0.0046.
Values may be sent and summed in bfloat16 or wider, within the bound.
A program may use at most 128 MiB of HBM per device.

```python
import math
import jax
import jax.numpy as jnp
from jax import lax

F = 4096
RAW = 256
TGT = 128
ROWS = 2048
ITERS = 2
FOLDS = 8


def with_ends(entries, rng, smallest, top_value):
    shape = entries.shape
    index_at = [jax.random.randint(jax.random.fold_in(rng, axis), (), 0, shape[axis]) for axis in range(len(shape))]
    entries = entries.at[tuple(index_at)].set(smallest)
    longest = shape.index(max(shape))
    index_at[longest] = (index_at[longest] + 1) % shape[longest]
    return entries.at[tuple(index_at)].set(top_value)


def levels(own_key, shape, split, low, top_value):
    loudness, own = 1.0, jax.random.fold_in(own_key, 6)
    for dim, blocks in split:
        steps = jnp.exp(jax.random.uniform(jax.random.fold_in(own, dim), (blocks,), jnp.float32, low / len(split), top_value / len(split)))
        loudness = loudness * jnp.repeat(steps, shape[dim] // blocks).reshape([-1 if axis == dim else 1 for axis in range(len(shape))])
    return loudness


def centred(rng, dims, scale, most, cuts=(), held_as=jnp.bfloat16):
    loudness = levels(rng, dims, cuts, -0.22, 0.18) if cuts else 1.0
    values = jax.random.normal(rng, dims, jnp.float32) * scale * loudness
    return jnp.minimum(jnp.maximum(values, -most), most).astype(held_as)


def setup_inputs(seed: int = 0) -> dict:
    key_of = jax.random.split(jax.random.key(seed), 9)
    return {
        "samples": centred(key_of[0], (FOLDS, ROWS, RAW), 1.0, 6.0, ((0, 4), (1, 8))),
        "targets": centred(key_of[1], (FOLDS, ROWS, TGT), 1.0, 6.0, ((0, 4), (1, 8))),
        "frequencies": centred(key_of[2], (RAW, F), (RAW // 16) ** -0.5, 1.5),
        "phases": jnp.clip(jax.random.uniform(key_of[3], (F,), jnp.float32, -3.140625, 3.140625), -3.140625, 3.140625),
        "valid_rows": with_ends(jax.random.randint(key_of[4], (FOLDS,), ROWS // 2, ROWS + 1), jax.random.fold_in(key_of[4], 1), ROWS // 2, ROWS).astype(jnp.int32),
        "ridge": jnp.clip(jnp.exp(math.log(1.0) - 2.3025851 * jax.random.uniform(key_of[5], (FOLDS,), jnp.float32) ** levels(key_of[5], (FOLDS,), ((0, 4),), -0.2, 0.2)), 0.1, 1.0),
        "low_bound": jnp.clip(0.05 + 0.35 * jax.random.uniform(key_of[6], (FOLDS,), jnp.float32) ** levels(key_of[6], (FOLDS,), ((0, 4),), -0.2, 0.2), 0.05, 0.4),
        "high_bound": jnp.clip(9.0 + 3.0 * jax.random.uniform(key_of[7], (FOLDS,), jnp.float32) ** levels(key_of[7], (FOLDS,), ((0, 4),), -0.2, 0.2), 9.0, 12.0),
    }


root_two = math.sqrt(2.0)

def reference(samples, targets, frequencies, phases, valid_rows, ridge, low_bound, high_bound):
    positions = jnp.arange(ROWS, dtype=jnp.int32)

    def advance(carry, item):
        gram_sum, cross_sum, count = carry
        sample_rows, target_rows, valid, shift, lower, upper = item
        angles = jnp.dot(sample_rows, frequencies, preferred_element_type=jnp.float32) + phases
        keep = (positions < valid).astype(jnp.float32)
        feats = (root_two * jnp.cos(angles) * keep[:, None]).astype(jnp.bfloat16)
        gram_sum = gram_sum + jnp.dot(feats.T, feats, preferred_element_type=jnp.float32)
        cross_sum = cross_sum + jnp.dot(feats.T, target_rows, preferred_element_type=jnp.float32)
        count = count + valid.astype(jnp.float32)
        matrix = gram_sum / count
        right_side = cross_sum / jnp.sqrt(count)
        center = (upper + lower) / 2.0 + shift
        spread = (upper - lower) / 2.0
        sigma = center / spread
        rho = 1.0 / sigma
        iterate = jnp.zeros_like(right_side)
        residual = right_side
        direction = right_side / center
        for turn in range(ITERS):
            iterate = iterate + direction
            image = jnp.dot(matrix, direction, precision=lax.Precision.HIGHEST) + shift * direction
            residual = residual - image
            rho_next = 1.0 / (2.0 * sigma - rho)
            direction = rho_next * rho * direction + 2.0 * rho_next / spread * residual
            rho = rho_next
        return ((gram_sum, cross_sum, count), (iterate, residual))
    start = (jnp.zeros((F, F), jnp.float32), jnp.zeros((F, TGT), jnp.float32), jnp.zeros((), jnp.float32))
    final, outputs = lax.scan(advance, start, (samples, targets, valid_rows, ridge, low_bound, high_bound))
    return (outputs[0], outputs[1])
```

```python
import math

import jax
import jax.numpy as jnp
import numpy as np
from jax import lax
from jax.sharding import PartitionSpec as P

ITERS = 2
SINE = (3.141582022142075, -5.16714279609351, 2.5418990253836506, -0.5546361920474749)


def pair_table(chips, cores):
    per = chips // (2 * cores)
    table = np.zeros((chips, cores, 2, per), np.int32)
    for z in range(chips):
        if z == 0:
            pairs = [(2 * per * c + i, 2 * per * c + per + i) for c in range(cores) for i in range(per)]
        else:
            pairs = [(a, a ^ z) for a in range(chips) if a < a ^ z]
        table[z] = np.array(pairs, np.int32).reshape(cores, per, 2).transpose(0, 2, 1)
    return table


def features(sample_rows, freq_cols, phase_cols, valid):
    angles = jnp.einsum("fkr,rc->fkc", sample_rows, freq_cols, preferred_element_type=jnp.float32)
    turn = np.float32(0.5 / math.pi)
    turns = angles * turn + phase_cols * turn
    rest = turns - jnp.round(turns)
    square = rest * rest
    poly = np.float32(SINE[3])
    for coef in SINE[2::-1]:
        poly = poly * square + np.float32(coef)
    sine = poly * rest * np.float32(2.0 ** 0.75)
    positions = lax.iota(jnp.int32, sample_rows.shape[1])
    keep = positions[None, :] < valid[:, None]
    return jnp.where(keep[:, :, None], np.float32(math.sqrt(2.0)) - sine * sine, 0.0).astype(jnp.bfloat16)


def fold_prefix(total, wire):
    size = lax.axis_size("fold")
    place = lax.axis_index("fold")
    earlier = jnp.zeros_like(total)
    step = 1
    while step < size:
        last = 2 * step >= size
        pairs = [(i, i ^ step) for i in range(size) if not (last and i & step)]
        got = lax.ppermute(total.astype(wire), "fold", pairs).astype(total.dtype)
        earlier = earlier + jnp.where((place & step) != 0, got, 0)
        total = total + got
        step *= 2
    return earlier


def halves(x):
    high = x.astype(jnp.bfloat16)
    return high, (x - high.astype(jnp.float32)).astype(jnp.bfloat16)


def product(spec, a, b):
    dot = lambda x, y: jnp.einsum(spec, x, y, preferred_element_type=jnp.float32)
    return dot(a[0], b[0]) + dot(a[0], b[1]) + dot(a[1], b[0])


def on_device(samples, targets, frequencies, phases, valid_rows, ridge, low_bound, high_bound):
    width = frequencies.shape[1]
    chips, cores = lax.axis_size("trow"), lax.axis_size("tcol")
    z, c = lax.axis_index("trow"), lax.axis_index("tcol")
    w = width // chips
    table = pair_table(chips, cores)
    per = table.shape[3]
    tgt = targets.shape[2]
    nf = samples.shape[0]
    ids = jnp.asarray(table)[z, c].reshape(2 * per)
    freq_cols = jnp.take(frequencies.reshape(-1, chips, w), ids, axis=1).reshape(-1, 2 * per * w)
    phase_cols = jnp.take(phases.reshape(chips, w), ids, axis=0).reshape(-1)
    rows = lax.all_gather(samples, ("trow", "tcol"), axis=1, tiled=True)
    target_rows = lax.all_gather(targets, ("trow", "tcol"), axis=1, tiled=True)
    feat = features(rows, freq_cols, phase_cols, valid_rows)
    feat = feat.reshape(nf, feat.shape[1], 2, per, w)
    left, right = feat[:, :, 0], feat[:, :, 1]
    counts = jnp.cumsum(valid_rows.astype(jnp.float32))

    part = w // chips
    mine = lax.dynamic_slice_in_dim(feat, z * part, part, 4)
    cross = jnp.einsum("fksaw,fkt->fsawt", mine, target_rows, preferred_element_type=jnp.float32)
    cross = jnp.cumsum(cross.reshape(nf, 2 * per, part, tgt), axis=0)
    cross = cross + fold_prefix(cross[-1], jnp.float32)[None]
    prefix_count = counts + fold_prefix(counts[-1:], jnp.float32)
    cross = cross / jnp.sqrt(prefix_count)[:, None, None, None]
    everyone = lax.all_gather(cross, ("trow", "tcol"), axis=0)
    everyone = jnp.moveaxis(everyone, 2, 1).reshape(-1, nf, part, tgt)
    source = np.zeros((chips, chips), np.int32)
    for k, block in enumerate(table.reshape(-1)):
        source[block, k // (cores * 2 * per)] = k
    right_side = jnp.take(everyone, source.reshape(-1), axis=0)
    right_side = jnp.moveaxis(right_side, 1, 0).reshape(nf, chips, w, tgt)

    diagonal = z == 0
    first = jnp.where(diagonal, left, right)
    second = jnp.where(diagonal, right, left)
    upper = lax.broadcasted_iota(jnp.int32, (w, w), 0) <= lax.broadcasted_iota(jnp.int32, (w, w), 1)
    same = jnp.eye(w, dtype=bool)
    gram_one = jnp.einsum("fkma,fkmb->fmab", left, first, preferred_element_type=jnp.float32)
    gram_two = jnp.einsum("fkma,fkmb->fmab", second, right, preferred_element_type=jnp.float32)
    half = jnp.where(jnp.logical_and(diagonal, same), 0.5, 1.0).astype(jnp.float32)
    tile = jnp.where(upper, gram_one, gram_two) * half
    own = jnp.where(diagonal, jnp.sum(right.astype(jnp.float32) ** 2, axis=1), 0.0)
    tile = jnp.cumsum(tile, axis=0)
    own = jnp.cumsum(own, axis=0)
    tile = (tile + fold_prefix(tile[-1], jnp.bfloat16)[None]) / prefix_count[:, None, None, None]
    own = (own + fold_prefix(own[-1], jnp.float32)[None]) / prefix_count[:, None, None]
    high, low = halves(tile)
    zero = jnp.zeros((), jnp.bfloat16)
    above = (jnp.where(upper, high, zero), jnp.where(upper, low, zero))
    below = (jnp.where(upper, zero, high), jnp.where(upper, zero, low))

    def apply(direction):
        mine = jnp.take(direction, ids, axis=1).reshape(nf, 2, per, w, tgt)
        dl, dr = mine[:, 0], mine[:, 1]
        hl, hr = halves(dl), halves(dr)
        pick = lambda a, b: tuple(jnp.where(diagonal, i, j) for i, j in zip(a, b))
        one = product("fmab,fmbt->fmat", above, pick(hl, hr))
        two = product("fmab,fmbt->fmat", below, hr)
        three = product("fmab,fmat->fmbt", above, hl)
        four = product("fmab,fmat->fmbt", below, pick(hr, hl))
        out_l = one + jnp.where(diagonal, three, two)
        out_r = four + jnp.where(diagonal, two, three) + own[..., None] * dr
        both = jnp.stack((out_l, out_r), 1).reshape(nf, 2 * per, w, tgt)
        both = lax.all_gather(both, "tcol", axis=1, tiled=True)
        chip_ids = jnp.asarray(table)[z].reshape(-1)
        order = jnp.argsort(chip_ids)
        wanted = lax.dynamic_slice_in_dim(order, c * (chips // cores), chips // cores, 0)
        return lax.psum(jnp.take(both, wanted, axis=1), "trow")

    expand = lambda x: x[:, None, None, None]
    share = chips // cores
    right_side_mine = lax.dynamic_slice_in_dim(right_side, c * share, share, 1)
    center = expand((high_bound + low_bound) / 2.0 + ridge)
    spread = expand((high_bound - low_bound) / 2.0)
    shift = expand(ridge)
    sigma = center / spread
    rho = 1.0 / sigma
    whole = right_side / center
    direction = right_side_mine / center
    iterate = jnp.zeros_like(direction)
    residual = right_side_mine
    for iteration in range(ITERS):
        iterate = iterate + direction
        residual = residual - (apply(whole) + shift * direction)
        if iteration + 1 < ITERS:
            rho_next = 1.0 / (2.0 * sigma - rho)
            direction = rho_next * rho * direction + 2.0 * rho_next / spread * residual
            rho = rho_next
            whole = lax.all_gather(direction, "tcol", axis=1, tiled=True)
    shape = (nf, share * w, tgt)
    return (iterate.reshape(shape), residual.reshape(shape))


def solution(mesh):
    in_specs = (
        P("fold", ("trow", "tcol"), None),
        P("fold", ("trow", "tcol"), None),
        P(),
        P(),
        P("fold"),
        P("fold"),
        P("fold"),
        P("fold"),
    )
    out_specs = (P("fold", "tcol", None), P("fold", "tcol", None))
    return jax.shard_map(
        on_device, mesh=mesh, in_specs=in_specs, out_specs=out_specs, check_vma=False
    )
```

```python
import math

import jax
import jax.numpy as jnp
import numpy as np
from jax import lax
from jax.experimental import pallas as pl
from jax.experimental.pallas import tpu as pltpu
from jax.sharding import PartitionSpec as P

ITERS = 2
ROW_BLOCK = 256
WIRE = jnp.float16
SINE = (3.141582022142075, -5.16714279609351, 2.5418990253836506, -0.5546361920474749)


def pair_table(chips, cores):
    per = chips // (2 * cores)
    table = np.zeros((chips, cores, 2, per), np.int32)
    for z in range(chips):
        if z == 0:
            pairs = [(2 * per * c + i, 2 * per * c + per + i) for c in range(cores) for i in range(per)]
        else:
            pairs = [(a, a ^ z) for a in range(chips) if a < a ^ z]
        table[z] = np.array(pairs, np.int32).reshape(cores, per, 2).transpose(0, 2, 1)
    return table


def features(sample_rows, freq_cols, phase_cols, valid):
    angles = jnp.einsum("fkr,rc->fkc", sample_rows, freq_cols, preferred_element_type=jnp.float32)
    turn = np.float32(0.5 / math.pi)
    turns = angles * turn + phase_cols * turn
    rest = turns - jnp.round(turns)
    square = rest * rest
    poly = np.float32(SINE[3])
    for coef in SINE[2::-1]:
        poly = poly * square + np.float32(coef)
    sine = poly * rest * np.float32(2.0 ** 0.75)
    positions = lax.iota(jnp.int32, sample_rows.shape[1])
    keep = positions[None, :] < valid[:, None]
    return jnp.where(keep[:, :, None], np.float32(math.sqrt(2.0)) - sine * sine, 0.0).astype(jnp.bfloat16)


def fold_prefix(total, wire):
    size = lax.axis_size("fold")
    place = lax.axis_index("fold")
    earlier = jnp.zeros_like(total)
    step = 1
    while step < size:
        last = 2 * step >= size
        pairs = [(i, i ^ step) for i in range(size) if not (last and i & step)]
        got = lax.ppermute(total.astype(wire), "fold", pairs).astype(total.dtype)
        earlier = earlier + jnp.where((place & step) != 0, got, 0)
        total = total + got
        step *= 2
    return earlier


def halves(x):
    high = x.astype(jnp.bfloat16)
    return high, (x - high.astype(jnp.float32)).astype(jnp.bfloat16)


def iterate_kernel(
    steps, rhs, own, above_hi, above_lo, below_hi, below_lo, iterate, residual,
    image, heading, inbox, cat, cat_t, prod, prod_t,
    core_send, core_recv, head_send, head_recv, chain_send, chain_recv,
):
    chips, cores = lax.axis_size("trow"), lax.axis_size("tcol")
    z, c = lax.axis_index("trow"), lax.axis_index("tcol")
    other = cores - 1 - c
    nf, share, w, tgt = iterate.shape
    table = pair_table(chips, cores)
    per = table.shape[3]
    block = min(w, ROW_BLOCK)
    mesh_id = pl.DeviceIdType.MESH
    f32, bf16 = jnp.float32, jnp.bfloat16
    diagonal = z == 0

    def lookup(core, side, i):
        found = jnp.int32(0)
        for place in range(chips):
            for one in range(cores):
                hit = jnp.logical_and(z == place, core == one)
                found = jnp.where(hit, jnp.int32(int(table[place, one, side, i])), found)
        return found

    mine = [lookup(c, side, i) for side in range(2) for i in range(per)]
    theirs = [lookup(other, side, i) for side in range(2) for i in range(per)]

    barrier = pltpu.get_barrier_semaphore()
    ways = ((z > 0, z - 1), (z < chips - 1, z + 1))
    pl.semaphore_signal(barrier, inc=1, device_id={"tcol": other}, device_id_type=mesh_id)
    for there, place in ways:
        @pl.when(there)
        def _():
            pl.semaphore_signal(barrier, inc=1, device_id={"trow": place}, device_id_type=mesh_id)
    peers = jnp.int32(1)
    for there, _ in ways:
        peers = peers + jnp.where(there, jnp.int32(1), jnp.int32(0))
    pl.semaphore_wait(barrier, peers)

    def to_core(ref, slot, send, recv):
        return pltpu.make_async_remote_copy(
            src_ref=ref.at[slot], dst_ref=ref.at[slot], send_sem=send, recv_sem=recv,
            device_id={"tcol": other}, device_id_type=mesh_id,
        )

    def hop(turn, way, f, j, i, source):
        place = (z + 1) if way == 0 else (z - 1)
        at = pl.ds(i * block, block)
        return pltpu.make_async_remote_copy(
            src_ref=source.at[at], dst_ref=inbox.at[turn, way, f, j, at],
            send_sem=chain_send.at[turn, way, f, j, i], recv_sem=chain_recv.at[turn, way, f, j, i],
            device_id={"trow": place}, device_id_type=mesh_id,
        )

    middle = chips // 2
    end = jnp.logical_or(z == 0, z == chips - 1)
    sides = ((z < middle, 0, z > 0, z == middle - 1), (z >= middle, 1, z < chips - 1, z == middle))

    def inward(turn, f, j, i):
        at = pl.ds(i * block, block)
        for here, way, outer, _ in sides:
            @pl.when(jnp.logical_and(here, outer))
            def _():
                hop(turn, way, f, j, i, inbox.at[turn, way, f, j]).wait_recv()
                image[turn, f, c * share + j, at] += inbox[turn, way, f, j, at]

            @pl.when(here)
            def _():
                hop(turn, way, f, j, i, image.at[turn, f, c * share + j]).start()

    def outward(turn, f, j, i):
        at = pl.ds(i * block, block)
        for here, way, outer, inner in sides:
            @pl.when(here)
            def _():
                hop(turn, 1 - way, f, j, i, inbox.at[turn, 1 - way, f, j]).wait_recv()

            @pl.when(inner)
            def _():
                inbox[turn, 1 - way, f, j, at] += image[turn, f, c * share + j, at]

            @pl.when(jnp.logical_and(here, outer))
            def _():
                hop(turn, 1 - way, f, j, i, inbox.at[turn, 1 - way, f, j]).start()

    def direction(turn, f, k):
        if turn == 0:
            return rhs[f, k] * steps[f, 0]
        return heading[turn - 1, f, k]

    def split(x):
        high = x.astype(bf16)
        return high, (x - high.astype(f32)).astype(bf16)

    def multiply(turn, f, m):
        dl, dr = direction(turn, f, mine[m]), direction(turn, f, mine[per + m])
        for k, x in enumerate((jnp.where(diagonal, dl, dr), dr)):
            high, low = split(x)
            cat[k, :, :tgt] = high
            cat[k, :, tgt:] = low
        for k, x in enumerate((dl, jnp.where(diagonal, dr, dl))):
            high, low = split(x.T)
            cat_t[k, :tgt, :] = high
            cat_t[k, tgt:, :] = low
        prod_t[...] = jnp.zeros_like(prod_t)

        def rows(i, carry):
            at = pl.ds(pl.multiple_of(i * block, block), block)
            for k, (hi, lo) in enumerate(((above_hi, above_lo), (below_hi, below_lo))):
                a, b = hi[f, m, at, :], lo[f, m, at, :]
                wide = jnp.dot(a, cat[k], preferred_element_type=f32)
                thin = jnp.dot(b, cat[k, :, :tgt], preferred_element_type=f32)
                prod[k, at, :] = wide[:, :tgt] + wide[:, tgt:] + thin
                d = cat_t[k, :, at]
                wide = jnp.dot(d, a, preferred_element_type=f32)
                thin = jnp.dot(d[:tgt], b, preferred_element_type=f32)
                prod_t[k] += wide[:tgt] + wide[tgt:] + thin
            return carry

        lax.fori_loop(0, w // block, rows, 0)
        three, four = prod_t[0].T, prod_t[1].T
        two = prod[1]
        image[turn, f, mine[m]] = prod[0] + jnp.where(diagonal, three, two)
        image[turn, f, mine[per + m]] = four + jnp.where(diagonal, two, three) + own[f, m] * dr

    iterate[...] = jnp.zeros_like(iterate)
    for f in range(nf):
        for j in range(share):
            residual[f, j] = rhs[f, c * share + j]
    for turn in range(ITERS):
        if turn > 0:
            for f in range(nf):
                for j in range(share):
                    to_core(heading, (turn - 1, f, other * share + j), head_send.at[turn, f, j], head_recv.at[turn, f, j]).wait_recv()
        for f in range(nf):
            for m in range(per):
                multiply(turn, f, m)
                for k in (m, per + m):
                    to_core(image, (turn, f, mine[k]), core_send.at[turn, f, k], core_recv.at[turn, f, k]).start()
        for f in range(nf):
            for k in range(2 * per):
                to_core(image, (turn, f, theirs[k]), core_send.at[turn, f, k], core_recv.at[turn, f, k]).wait_recv()
        for f in range(nf):
            for k in range(2 * per):
                to_core(image, (turn, f, mine[k]), core_send.at[turn, f, k], core_recv.at[turn, f, k]).wait_send()
        pieces = [(f, j, i) for f in range(nf) for j in range(share) for i in range(w // block)]

        @pl.when(end)
        def _():
            for piece in pieces:
                inward(turn, *piece)

        for f in range(nf):
            for j in range(share):
                for i in range(w // block):
                    @pl.when(jnp.logical_not(end))
                    def _():
                        inward(turn, f, j, i)

                    outward(turn, f, j, i)
                total = inbox[turn, jnp.where(z < middle, jnp.int32(1), jnp.int32(0)), f, j]
                now = direction(turn, f, c * share + j)
                iterate[f, j] = iterate[f, j] + now
                left = residual[f, j] - (total + steps[f, 1] * now)
                residual[f, j] = left
                if turn + 1 < ITERS:
                    heading[turn, f, c * share + j] = steps[f, 2 + 2 * turn] * now + steps[f, 3 + 2 * turn] * left
                    to_core(heading, (turn, f, c * share + j), head_send.at[turn + 1, f, j], head_recv.at[turn + 1, f, j]).start()
    for turn in range(ITERS):
        for f in range(nf):
            for j in range(share):
                if turn > 0:
                    to_core(heading, (turn - 1, f, c * share + j), head_send.at[turn, f, j], head_recv.at[turn, f, j]).wait_send()
                for i in range(w // block):
                    for here, way, outer, _ in sides:
                        @pl.when(here)
                        def _():
                            hop(turn, way, f, j, i, image.at[turn, f, c * share + j]).wait_send()

                        @pl.when(jnp.logical_and(here, outer))
                        def _():
                            hop(turn, 1 - way, f, j, i, inbox.at[turn, 1 - way, f, j]).wait_send()


def on_device(samples, targets, frequencies, phases, valid_rows, ridge, low_bound, high_bound):
    width = frequencies.shape[1]
    chips, cores = lax.axis_size("trow"), lax.axis_size("tcol")
    z, c = lax.axis_index("trow"), lax.axis_index("tcol")
    w = width // chips
    table = pair_table(chips, cores)
    per = table.shape[3]
    tgt = targets.shape[2]
    nf = samples.shape[0]
    ids = jnp.asarray(table)[z, c].reshape(2 * per)
    freq_cols = jnp.take(frequencies.reshape(-1, chips, w), ids, axis=1).reshape(-1, 2 * per * w)
    phase_cols = jnp.take(phases.reshape(chips, w), ids, axis=0).reshape(-1)
    rows = lax.all_gather(samples, ("trow", "tcol"), axis=1, tiled=True)
    target_rows = lax.all_gather(targets, ("trow", "tcol"), axis=1, tiled=True)
    feat = features(rows, freq_cols, phase_cols, valid_rows)
    feat = feat.reshape(nf, feat.shape[1], 2, per, w)
    left, right = feat[:, :, 0], feat[:, :, 1]
    counts = jnp.cumsum(valid_rows.astype(jnp.float32))

    part = w // chips
    mine = lax.dynamic_slice_in_dim(feat, z * part, part, 4)
    cross = jnp.einsum("fksaw,fkt->fsawt", mine, target_rows, preferred_element_type=jnp.float32)
    cross = jnp.cumsum(cross.reshape(nf, 2 * per, part, tgt), axis=0)
    cross = cross + fold_prefix(cross[-1], jnp.float32)[None]
    prefix_count = counts + fold_prefix(counts[-1:], jnp.float32)
    cross = cross / jnp.sqrt(prefix_count)[:, None, None, None]
    everyone = lax.all_gather(cross, ("trow", "tcol"), axis=0)
    everyone = jnp.moveaxis(everyone, 2, 1).reshape(-1, nf, part, tgt)
    source = np.zeros((chips, chips), np.int32)
    for k, block in enumerate(table.reshape(-1)):
        source[block, k // (cores * 2 * per)] = k
    right_side = jnp.take(everyone, source.reshape(-1), axis=0)
    right_side = jnp.moveaxis(right_side, 1, 0).reshape(nf, chips, w, tgt)

    diagonal = z == 0
    first = jnp.where(diagonal, left, right)
    second = jnp.where(diagonal, right, left)
    own = jnp.where(diagonal, jnp.sum(right.astype(jnp.float32) ** 2, axis=1), 0.0)
    own = jnp.cumsum(own, axis=0)
    own = (own + fold_prefix(own[-1], jnp.float32)[None]) / prefix_count[:, None, None]
    block = min(w, ROW_BLOCK)
    upper = lax.broadcasted_iota(jnp.int32, (block, block), 0) <= lax.broadcasted_iota(jnp.int32, (block, block), 1)
    half = jnp.where(jnp.logical_and(diagonal, jnp.eye(block, dtype=bool)), 0.5, 1.0).astype(jnp.float32)
    most = 2.1 * nf * lax.axis_size("fold") * rows.shape[1]
    fit = np.float32(2.0 ** min(0, math.floor(math.log2(60000.0 / most))))
    parts = ([], [], [], [])
    for start in range(0, w, block):
        stop = start + block
        one = jnp.einsum("fkma,fkmb->fmab", left[..., start:stop], first[..., start:], preferred_element_type=jnp.float32)
        two = jnp.einsum("fkma,fkmb->fmab", second[..., start:stop], right[..., :stop], preferred_element_type=jnp.float32)
        middle = jnp.where(upper, one[..., :block], two[..., start:]) * half
        tile = jnp.concatenate((two[..., :start], middle, one[..., block:]), axis=3)
        tile = jnp.cumsum(tile, axis=0)
        tile = (tile + fold_prefix(tile[-1] * fit, WIRE)[None] / fit) / prefix_count[:, None, None, None]
        above = (lax.broadcasted_iota(jnp.int32, (block, w), 0) + start) <= lax.broadcasted_iota(jnp.int32, (block, w), 1)
        high, low = halves(tile)
        zero = jnp.zeros((), jnp.bfloat16)
        for k, x in enumerate((high, low)):
            parts[k].append(jnp.where(above, x, zero))
            parts[2 + k].append(jnp.where(above, zero, x))
    matrices = [jnp.concatenate(x, axis=2) for x in parts]

    center = (high_bound + low_bound) / 2.0 + ridge
    spread = (high_bound - low_bound) / 2.0
    sigma = center / spread
    rho = 1.0 / sigma
    steps = [1.0 / center, ridge]
    for iteration in range(ITERS - 1):
        rho_next = 1.0 / (2.0 * sigma - rho)
        steps += [rho_next * rho, 2.0 * rho_next / spread]
        rho = rho_next
    steps = jnp.stack(steps, axis=1)
    share = chips // cores
    own = jnp.broadcast_to(own[..., None], own.shape + (tgt,))
    block_shape = (nf, share, w, tgt)
    vmem = pl.BlockSpec(memory_space=pltpu.VMEM)
    f32, bf16 = jnp.float32, jnp.bfloat16
    dma = pltpu.SemaphoreType.DMA
    iterate, residual = pl.pallas_call(
        iterate_kernel,
        out_shape=[jax.ShapeDtypeStruct(block_shape, f32)] * 2,
        in_specs=[pl.BlockSpec(memory_space=pltpu.SMEM)] + [vmem] * 6,
        out_specs=[vmem] * 2,
        scratch_shapes=[
            pltpu.VMEM((ITERS, nf, chips, w, tgt), f32),
            pltpu.VMEM((max(ITERS - 1, 1), nf, chips, w, tgt), f32),
            pltpu.VMEM((ITERS, 2, nf, share, w, tgt), f32),
            pltpu.VMEM((2, w, 2 * tgt), bf16),
            pltpu.VMEM((2, 2 * tgt, w), bf16),
            pltpu.VMEM((2, w, tgt), f32),
            pltpu.VMEM((2, tgt, w), f32),
            dma((ITERS, nf, 2 * per)),
            dma((ITERS, nf, 2 * per)),
            dma((ITERS, nf, share)),
            dma((ITERS, nf, share)),
            dma((ITERS, 2, nf, share, w // block)),
            dma((ITERS, 2, nf, share, w // block)),
        ],
        compiler_params=pltpu.CompilerParams(
            collective_id=0, has_side_effects=True, vmem_limit_bytes=60 * 2**20
        ),
        name="iterations",
    )(steps, right_side, own, *matrices)
    shape = (nf, share * w, tgt)
    return (iterate.reshape(shape), residual.reshape(shape))


def solution(mesh):
    in_specs = (
        P("fold", ("trow", "tcol"), None),
        P("fold", ("trow", "tcol"), None),
        P(),
        P(),
        P("fold"),
        P("fold"),
        P("fold"),
        P("fold"),
    )
    out_specs = (P("fold", "tcol", None), P("fold", "tcol", None))
    return jax.shard_map(
        on_device, mesh=mesh, in_specs=in_specs, out_specs=out_specs, check_vma=False
    )
```
